32 devices in a mesh: groups: 2 (over y), rows: 16 (over z, x, core).
Axes of the slice: x: 2, y: 2, z: 4, core: 2. Of those that a mesh axis runs over, the one named last changes fastest.
Arguments:
- tiles: bfloat16 [16, 12, 128, 128], P('rows'), may hold values from -0.15625 to 0.15625
- column_ids: int32 [16, 12], P('rows'), may hold values from 0 to 15, all different within a row
- costs: float32 [32, 30, 128], P(('groups', 'rows')), parts along dimension 0, may hold values from -6 to 6
- upper: float32 [32, 30, 128], P(('groups', 'rows')), parts along dimension 0, may hold values from 0.5 to 4
- demand: float32 [32, 30, 128], P(('groups', 'rows')), parts along dimension 0, may hold values from -6 to 6
- x_start: float32 [32, 30, 128], P(('groups', 'rows')), parts along dimension 0, may hold values from 0 to 0.5
- y_start: float32 [32, 30, 128], P(('groups', 'rows')), parts along dimension 0, may hold values from -6 to 6
- row_weight: float32 [16, 128], P('rows'), may hold values from 0.1 to 1
- area_of_row: int32 [2048], P('rows'), may hold values from 0 to 63, never falling along the last dimension, each value on 1 to 64 neighbouring positions
Outputs:
- x_avg: float32 [32, 30, 128], P(('groups', 'rows')), parts along dimension 0
- y_avg: float32 [32, 30, 128], P(('groups', 'rows')), parts along dimension 0
- area_prices: float32 [128, 30], P('groups'), parts along dimension 0
- primal_weight: float32 [60], P('groups'), parts along dimension 0
The draws below stay inside these ranges and needn't reach their ends.
There are 2 independent parts, one for each index of `groups`. The reference program is written for one: setup_inputs(seed, part) draws one part's arguments, and reference() takes and returns one part's arrays. A program takes and returns all parts, laid end to end along the dimension named above; an argument that names none is the same for every part. Nothing has to cross between parts.
Inputs may be any that keep to these rules, and one draw needn't show every extreme that they name: `column_ids`: each row block names 12 different column blocks; every column block is named by some row block. `area_of_row`: area numbers never fall along the rows, and every area has a row.
All inputs are finite; a program needn't handle non-finite values.
Results may differ from the reference program's by a relative error of at most 0.0011.
Values may be sent and summed in bfloat16 or wider, within the bound.
A program may use at most 64 MiB of HBM per device.

```python
import math
import jax
import jax.numpy as jnp
import numpy as np
from jax import lax

TILE = 128
S = 30
ITERS = 4
AREAS = 64
NCB = 16
NRB = 16
K = 12


def shard_levels(rng, shape, cuts, low, top_value):
    level, own = 1.0, jax.random.fold_in(rng, 6)
    for position, blocks in cuts:
        steps = jnp.exp(jax.random.uniform(jax.random.fold_in(own, position), (blocks,), jnp.float32, low / len(cuts), top_value / len(cuts)))
        level = level * jnp.repeat(steps, shape[position] // blocks).reshape([-1 if axis == position else 1 for axis in range(len(shape))])
    return level


def different_ones(key, rows, number_of, top, lift):
    sequence = jax.random.permutation(jax.random.fold_in(key, 1), number_of)
    pull = sequence
    for power in range(3):
        pull = pull * pull // number_of
    pull = pull * lift // number_of
    lots = jax.random.randint(jax.random.fold_in(key, 2), (rows, number_of), 0, 4096) + pull
    fixed_rows = jax.random.permutation(jax.random.fold_in(key, 3), rows)[jnp.arange(number_of) % rows]
    lots = jnp.where(jnp.arange(rows)[:, None] == fixed_rows[None, :], 1 << 14, lots)
    merit = lots * number_of + jnp.arange(number_of)
    return lax.top_k(merit.astype(jnp.int32), top)[1].astype(jnp.int32)


def length_profile(number_of, total, most, skew):
    loads = [(1 << 20) // math.isqrt(standing ** skew) + 1 for standing in range(2, number_of + 1)]
    rest, counts = total - most - (number_of - 1), [1] * (number_of - 1)
    while rest > 0:
        movable = [i for i in range(number_of - 1) if counts[i] < most]
        whole, remaining = sum([loads[i] for i in movable]), rest
        for i in movable:
            addition = min(most - counts[i], max(1, remaining * loads[i] // whole), rest)
            counts[i] = counts[i] + addition
            rest = rest - addition
    return np.array([most] + counts)


def ragged(key, amount, total, most, slope):
    if amount == 2:
        one = jax.random.randint(key, (), max(1, total - most), min(most, total - 1) + 1)
        return jnp.stack([one, total - one])
    sizes = jnp.asarray(length_profile(amount, total, most, slope), jnp.int32)
    couples = (amount - 1) // 2
    giver, taker = sizes[1:1 + 2 * couples:2], sizes[2:2 + 2 * couples:2]
    room = jnp.minimum(giver - 1, most - taker)
    moved = jax.random.randint(jax.random.fold_in(key, 1), (couples,), 0, 1 << 20) % (room + 1)
    sizes = sizes.at[1:1 + 2 * couples:2].set(giver - moved).at[2:2 + 2 * couples:2].set(taker + moved)
    return sizes[jax.random.permutation(jax.random.fold_in(key, 2), amount)]


def normal_values(rng, extent, spread, most, shards=(), kind=jnp.bfloat16):
    loudness = shard_levels(rng, extent, shards, -0.22, 0.18) if shards else 1.0
    result = jax.random.normal(rng, extent, jnp.float32) * spread * loudness
    return jnp.minimum(jnp.maximum(result, -most), most).astype(kind)


def setup_inputs(seed: int = 0, part: int = 0) -> dict:
    arg_keys = jax.random.split(jax.random.key(seed), 10)
    part_keys = jax.random.split(jax.random.fold_in(arg_keys[9], part), 10)
    return {
        "tiles": normal_values(arg_keys[0], (NRB, K, TILE, TILE), (K * TILE) ** -0.5, 0.15625, ((0, 16),)),
        "column_ids": different_ones(arg_keys[1], NRB, NCB, K, 0),
        "costs": normal_values(part_keys[2], (NCB, S, TILE), 1.0, 6.0, ((0, 16),), jnp.float32),
        "upper": jnp.clip(jnp.exp(math.log(4.0) - 2.0794415 * jax.random.uniform(part_keys[3], (NCB, S, TILE), jnp.float32) ** shard_levels(part_keys[3], (NCB, S, TILE), ((0, 16),), -0.2, 0.2)), 0.5, 4.0),
        "demand": normal_values(part_keys[4], (NRB, S, TILE), 1.0, 6.0, ((0, 16),), jnp.float32),
        "x_start": jnp.clip(0.5 * jax.random.uniform(part_keys[5], (NCB, S, TILE), jnp.float32) ** shard_levels(part_keys[5], (NCB, S, TILE), ((0, 16),), -0.2, 0.2), 0.0, 0.5),
        "y_start": normal_values(part_keys[6], (NRB, S, TILE), 1.0, 6.0, ((0, 16),), jnp.float32),
        "row_weight": jnp.clip(jnp.exp(math.log(1.0) - 2.3025851 * jax.random.uniform(arg_keys[7], (NRB, TILE), jnp.float32) ** shard_levels(arg_keys[7], (NRB, TILE), ((0, 16),), -0.2, 0.2)), 0.1, 1.0),
        "area_of_row": jnp.searchsorted(jnp.cumsum(ragged(arg_keys[8], AREAS, NRB * TILE, 2 * NRB * TILE // AREAS, 1)), jnp.arange(NRB * TILE), side="right").astype(jnp.int32),
    }


primal_step = 0.3
dual_step = 0.3
small_eps = 1e-06

def apply_matrix(tiles, column_ids, points):

    def one_block(args):
        block, ids = args
        picked = points[ids].astype(jnp.float32)
        return jnp.einsum('kij,ksj->si', block.astype(jnp.float32), picked, precision=lax.Precision.HIGHEST)
    return lax.map(one_block, (tiles, column_ids))

def apply_transpose(tiles, column_ids, duals):

    def add_block(total, args):
        block, ids, dual = args
        part = jnp.einsum('kij,si->ksj', block.astype(jnp.float32), dual.astype(jnp.float32), precision=lax.Precision.HIGHEST)
        return (total.at[ids].add(part), None)
    start = jnp.zeros((NCB, S, TILE), jnp.float32)
    return lax.scan(add_block, start, (tiles, column_ids, duals))[0]

def reference(tiles, column_ids, costs, upper, demand, x_start, y_start, row_weight, area_of_row):
    primal = x_start
    dual = y_start
    sum_x = jnp.zeros_like(x_start)
    sum_y = jnp.zeros_like(y_start)
    for step in range(ITERS):
        grad = costs - apply_transpose(tiles, column_ids, dual.astype(jnp.bfloat16))
        x_next = jnp.clip(primal - primal_step * grad, 0.0, upper)
        x_bar = (2.0 * x_next - primal).astype(jnp.bfloat16)
        dual = dual + dual_step * (demand - apply_matrix(tiles, column_ids, x_bar))
        primal = x_next
        sum_x = sum_x + primal
        sum_y = sum_y + dual
    x_avg = sum_x / ITERS
    y_avg = sum_y / ITERS
    delta_x = lax.optimization_barrier(jnp.sum((x_avg - x_start) ** 2, axis=(0, 2)))
    delta_y = lax.optimization_barrier(jnp.sum((y_avg - y_start) ** 2, axis=(0, 2)))
    primal_weight = jnp.sqrt((delta_y + small_eps) / (delta_x + small_eps))
    onehot = (area_of_row[None, :] == jnp.arange(AREAS, dtype=jnp.int32)[:, None]).astype(jnp.float32)
    weighted = row_weight[:, None, :] * y_avg
    numer = jnp.einsum('art,rst->as', onehot.reshape(AREAS, NRB, TILE), weighted, precision=lax.Precision.HIGHEST)
    denom = jnp.dot(onehot, row_weight.reshape(-1), precision=lax.Precision.HIGHEST)
    area_prices = numer / denom[:, None]
    return (x_avg, y_avg, area_prices, primal_weight)
```

```python
import functools

import jax
import jax.numpy as jnp
from jax import lax
from jax.experimental import pallas as pl
from jax.experimental.pallas import tpu as pltpu
from jax.sharding import PartitionSpec as P

ITERS = 4
AREAS = 64
LANES = 128

primal_step = 0.3
dual_step = 0.3
small_eps = 1e-06

NT = (((1,), (1,)), ((), ()))


def fold(lo, hi, body, carry):
    if hi - lo <= 32:
        for d in range(lo, hi):
            carry = body(d, carry)
        return carry
    return lax.fori_loop(lo, hi, body, carry)


def each(lo, hi, body):
    def step(d, carry):
        body(d)
        return carry

    fold(lo, hi, step, 0)


def block_at(d):
    start = d * LANES
    if not isinstance(d, int):
        start = pl.multiple_of(start, LANES)
    return pl.ds(start, LANES)


def kernel(
    n, tiles, ids, costs, upper, demand, x_start, y_start, row_weight, area,
    x_out, y_out, price_out, weight_out,
    dense, part_send, part_recv, bar_buf, last_send, last_recv,
    send_sems, recv_sems,
):
    me = lax.axis_index("rows")
    count = tiles.shape[1]
    s = costs.shape[1]
    sp = bar_buf.shape[2]

    def peer(d):
        return {"rows": lax.rem(me + d, n)}

    def send(src, dst, phase, where):
        pltpu.make_async_remote_copy(
            src_ref=src, dst_ref=dst, send_sem=send_sems.at[phase], recv_sem=recv_sems.at[phase],
            device_id=where, device_id_type=pl.DeviceIdType.MESH,
        ).start()

    def wait(ref, sem):
        pltpu.make_async_copy(ref, ref, sem).wait()

    barrier = pltpu.get_barrier_semaphore()
    each(1, n, lambda d: pl.semaphore_signal(
        barrier, inc=1, device_id=peer(d), device_id_type=pl.DeviceIdType.MESH))

    def place(d):
        column = lax.rem(me + d, n)

        def look(k, found):
            return jnp.where(ids[0, k] == column, k, found)

        found = fold(0, count, look, jnp.int32(-1))
        tile = tiles[0, jnp.maximum(found, 0)]
        dense[:, block_at(d)] = jnp.where(found >= 0, tile, jnp.zeros_like(tile))

    each(0, n, place)

    def padded(ref):
        return jnp.concatenate([ref[0], jnp.zeros((sp - s, LANES), jnp.float32)], axis=0)

    cost, top, need, first_x, first_y = map(padded, (costs, upper, demand, x_start, y_start))
    x, y = first_x, first_y
    sum_x = jnp.zeros_like(x)
    sum_y = jnp.zeros_like(y)
    pl.semaphore_wait(barrier, n - 1)

    for t in range(ITERS):
        y_round = y.astype(jnp.bfloat16)

        def term(d):
            return jnp.dot(y_round, dense[:, block_at(d)], preferred_element_type=jnp.float32)

        def send_part(d):
            part_send[t, d - 1] = term(d)
            send(part_send.at[t, d - 1], part_recv.at[t, d - 1], 2 * t, peer(d))

        each(1, n, send_part)
        own = term(0)
        wait(part_recv.at[t], recv_sems.at[2 * t])
        product = fold(0, n - 1, lambda d, total: total + part_recv[t, d], own)
        x_next = jnp.clip(x - primal_step * (cost - product), 0.0, top)
        bar_buf[t, 0] = (2.0 * x_next - x).astype(jnp.bfloat16)
        each(1, n, lambda d: send(bar_buf.at[t, 0], bar_buf.at[t, d], 2 * t + 1, peer(n - d)))
        x = x_next
        sum_x = sum_x + x
        if t == ITERS - 1:
            x_avg = sum_x / ITERS
            x_out[0] = x_avg[:s]
        wait(bar_buf.at[t, pl.ds(1, n - 1)], recv_sems.at[2 * t + 1])
        if n <= 32:
            whole = jnp.concatenate([bar_buf[t, d] for d in range(n)], axis=1)
            product = lax.dot_general(whole, dense[...], NT, preferred_element_type=jnp.float32)
        else:
            product = fold(0, n, lambda d, total: total + lax.dot_general(
                bar_buf[t, d], dense[:, block_at(d)], NT, preferred_element_type=jnp.float32),
                jnp.zeros_like(y))
        y = y + dual_step * (need - product)
        sum_y = sum_y + y

    y_avg = sum_y / ITERS
    y_out[0] = y_avg[:s]
    rows = lax.broadcasted_iota(jnp.int32, (sp, LANES), 0)
    weighted = row_weight[...] * jnp.where(rows == s, 1.0, y_avg)
    onehot = (lax.broadcasted_iota(jnp.int32, (AREAS, LANES), 0) == area[...]).astype(jnp.float32)
    sums = lax.dot_general(weighted, onehot, NT, precision=lax.Precision.HIGHEST,
                           preferred_element_type=jnp.float32)
    squares = jnp.concatenate([(x_avg - first_x) ** 2, (y_avg - first_y) ** 2], axis=0)
    steps = lax.dot_general(jnp.ones((8, LANES), jnp.float32), squares, NT,
                            precision=lax.Precision.HIGHEST, preferred_element_type=jnp.float32)
    sums = jnp.where(rows[:, :AREAS] == s + 1, steps[:1], sums)
    half = sp // 2
    last_send[...] = jnp.concatenate([sums[:half], sums[half:]], axis=1)
    last = 2 * ITERS
    each(1, n, lambda d: send(last_send, last_recv.at[me], last, peer(d)))
    last_recv[me] = last_send[...]
    wait(last_recv.at[pl.ds(0, n - 1)], recv_sems.at[last])
    total = fold(1, n, lambda d, total: total + last_recv[d], last_recv[0])
    sums = jnp.concatenate([total[:, :AREAS], total[:, AREAS:]], axis=0)
    price = sums / sums[s:s + 1]
    price_out[...] = price.T[:, :s]
    ends = sums[s + 1:s + 2] + small_eps
    weight_out[...] = jnp.sqrt(ends[:, sp:sp + s] / ends[:, :s])

    for t in range(ITERS):
        wait(part_send.at[t], send_sems.at[2 * t])
        wait(bar_buf.at[t, pl.ds(1, n - 1)], send_sems.at[2 * t + 1])
    wait(last_recv.at[pl.ds(0, n - 1)], send_sems.at[last])


def per_device(n, tiles, column_ids, costs, upper, demand, x_start, y_start, row_weight, area):
    s = costs.shape[1]
    sp = -(-(s + 2) // 16) * 16
    f32 = jnp.float32
    vmem = pl.BlockSpec(memory_space=pltpu.VMEM)
    x_avg, y_avg, price, weight = pl.pallas_call(
        functools.partial(kernel, n),
        out_shape=(
            jax.ShapeDtypeStruct(x_start.shape, f32),
            jax.ShapeDtypeStruct(y_start.shape, f32),
            jax.ShapeDtypeStruct((AREAS, s), f32),
            jax.ShapeDtypeStruct((1, s), f32),
        ),
        in_specs=[vmem, pl.BlockSpec(memory_space=pltpu.SMEM)] + [vmem] * 7,
        out_specs=[vmem] * 4,
        scratch_shapes=[
            pltpu.VMEM((LANES, n * LANES), jnp.bfloat16),
            pltpu.VMEM((ITERS, n - 1, sp, LANES), f32),
            pltpu.VMEM((ITERS, n - 1, sp, LANES), f32),
            pltpu.VMEM((ITERS, n, sp, LANES), jnp.bfloat16),
            pltpu.VMEM((sp // 2, LANES), f32),
            pltpu.VMEM((n, sp // 2, LANES), f32),
            pltpu.SemaphoreType.DMA((2 * ITERS + 1,)),
            pltpu.SemaphoreType.DMA((2 * ITERS + 1,)),
        ],
        compiler_params=pltpu.CompilerParams(
            collective_id=0, has_side_effects=True, vmem_limit_bytes=44 * 2**20
        ),
    )(tiles, column_ids, costs, upper, demand, x_start, y_start, row_weight, area.reshape(1, -1))
    return x_avg, y_avg, price, weight.reshape(s)


def solution(mesh):
    case = P(("groups", "rows"), None, None)
    in_specs = (
        P("rows", None, None, None), P("rows", None), case, case, case, case, case,
        P("rows", None), P("rows"),
    )
    out_specs = (case, case, P("groups", None), P("groups"))
    return jax.shard_map(
        functools.partial(per_device, mesh.shape["rows"]),
        mesh=mesh, in_specs=in_specs, out_specs=out_specs, check_vma=False,
    )
```

```python
import functools

import jax
import jax.numpy as jnp
from jax import lax
from jax.experimental import pallas as pl
from jax.experimental.pallas import tpu as pltpu
from jax.sharding import PartitionSpec as P

ITERS = 4
AREAS = 64
LANES = 128

primal_step = 0.3
dual_step = 0.3
small_eps = 1e-06

NT = (((1,), (1,)), ((), ()))
FULL = lax.Precision.HIGHEST


def fold(lo, hi, body, carry):
    if hi - lo <= 32:
        for d in range(lo, hi):
            carry = body(d, carry)
        return carry
    return lax.fori_loop(lo, hi, body, carry)


def each(lo, hi, body):
    def step(d, carry):
        body(d)
        return carry

    fold(lo, hi, step, 0)


def block_at(d, width=LANES):
    start = d * width
    if not isinstance(start, int):
        start = pl.multiple_of(start, LANES)
    return pl.ds(start, width)


def flipped(number, mask, count):
    result, bit = 0, 1
    while bit < count:
        b = lax.rem(lax.div(number, bit), 2)
        if isinstance(mask, int):
            b = 1 - b if mask // bit % 2 else b
        else:
            m = lax.rem(lax.div(mask, bit), 2)
            b = b + m - 2 * b * m
        result = result + b * bit
        bit = 2 * bit
    return result


def kernel(
    n, tiles_in, ids, costs, upper, demand, x_start, y_start, row_weight, area,
    x_out, y_out, price_out, weight_out,
    tiles, cases, small, dense, stage, start_send, start_recv, part_send, part_recv, bar_buf,
    swap_send, swap_recv, step_send, step_recv, last_send, last_recv,
    in_sems, send_sems, recv_sems,
):
    me = lax.axis_index("rows")
    core = lax.rem(me, 2)
    chip = lax.div(me, 2)
    chips = n // 2
    count = tiles_in.shape[1]
    s = costs.shape[0]
    sp = bar_buf.shape[2]
    f32 = jnp.float32
    sibling = {"rows": me + 1 - 2 * core}
    PART, BAR, SWAP = 0, ITERS, 2 * ITERS
    START, MATRIX, STEP, LAST = (3 * ITERS + i for i in range(4))

    def peer(m):
        return {"rows": 2 * flipped(chip, m, chips) + core}

    def remote(src, dst, phase, where):
        return pltpu.make_async_remote_copy(
            src_ref=src, dst_ref=dst, send_sem=send_sems.at[phase], recv_sem=recv_sems.at[phase],
            device_id=where, device_id_type=pl.DeviceIdType.MESH,
        )

    def wait(ref, sem):
        pltpu.make_async_copy(ref, ref, sem).wait()

    def signal(where):
        pl.semaphore_signal(barrier, inc=1, device_id=where, device_id_type=pl.DeviceIdType.MESH)

    barrier = pltpu.get_barrier_semaphore()
    loads = [pltpu.make_async_copy(tiles_in.at[0], tiles, in_sems.at[0])]
    for i, ref in enumerate((costs, upper, demand, x_start, y_start)):
        loads.append(pltpu.make_async_copy(
            ref.at[:, 0], cases.at[i, pl.ds(0, s)], in_sems.at[1 + i]))
    loads.append(pltpu.make_async_copy(row_weight, small.at[0], in_sems.at[6]))
    loads.append(pltpu.make_async_copy(area, small.at[1], in_sems.at[7]))
    for load in loads:
        load.start()
    each(1, chips, lambda d: signal(peer(chips - d)))
    signal(sibling)
    cases[:, s:] = jnp.zeros((5, sp - s, LANES), f32)

    def find(column):
        return fold(0, count, lambda k, found: jnp.where(ids[0, k] == column, k, found),
                    jnp.int32(-1))

    for load in loads:
        load.wait()
    cost, top, first_x = cases[0], cases[1], cases[3]
    start_send[0] = cases[2]
    start_send[1] = cases[4]
    start_send[1, s:s + 1] = small[0]
    start_send[1, s + 1:s + 2] = small[1]

    def place(m):
        other = flipped(chip, m, chips)
        for target, number in ((dense, core), (stage, 1 - core)):
            found = find(2 * other + number)
            tile = tiles[jnp.maximum(found, 0)]
            target[0:LANES, block_at(m)] = jnp.where(found >= 0, tile, jnp.zeros_like(tile))

    each(0, chips, place)
    pl.semaphore_wait(barrier, chips)
    remote(stage, dense.at[pl.ds(LANES, LANES)], MATRIX, sibling).start()
    remote(start_send, start_recv, START, sibling).start()

    rows = lax.broadcasted_iota(jnp.int32, (sp, LANES), 0)
    real = rows < s
    need = (cases[2], None)
    first_y = (cases[4], None)
    x = first_x
    sum_x = jnp.zeros_like(x)
    wait(start_recv, recv_sems.at[START])
    need = (cases[2], start_recv[0])
    first_y = (cases[4], jnp.where(real, start_recv[1], 0.0))
    y = first_y
    sum_y = (jnp.zeros_like(x), jnp.zeros_like(x))
    wait(stage, recv_sems.at[MATRIX])

    for t in range(ITERS):
        y_round = jnp.concatenate(y, axis=1).astype(jnp.bfloat16)

        def send_part(i):
            pair = chips // 2 - 1 - i
            both = jnp.dot(y_round, dense[:, block_at(pair, 2 * LANES)],
                           preferred_element_type=f32)
            for m, value in ((2 * pair + 1, both[:, LANES:]), (2 * pair, both[:, :LANES])):
                part_send[t, m] = value
                remote(part_send.at[t, m], part_recv.at[t, m], PART + t, peer(m)).start()

        each(0, chips // 2 - 1, send_part)
        both = jnp.dot(y_round, dense[:, 0:2 * LANES], preferred_element_type=f32)
        part_send[t, 1] = both[:, LANES:]
        remote(part_send.at[t, 1], part_recv.at[t, 1], PART + t, peer(1)).start()
        others = pl.ds(1, chips - 1)
        wait(part_recv.at[t, others], recv_sems.at[PART + t])
        product = fold(1, chips, lambda m, total: total + part_recv[t, m], both[:, :LANES])
        x_next = jnp.clip(x - primal_step * (cost - product), 0.0, top)
        bar_buf[t, 0] = (2.0 * x_next - x).astype(jnp.bfloat16)
        each(1, chips, lambda d: remote(
            bar_buf.at[t, 0], bar_buf.at[t, chips - d], BAR + t, peer(chips - d)).start())
        x = x_next
        sum_x = sum_x + x
        if t == ITERS - 1:
            x_avg = sum_x / ITERS
            x_out[0] = x_avg[:s]
            steps = lax.dot_general(jnp.ones((8, LANES), f32), (x_avg - first_x) ** 2, NT,
                                    precision=FULL, preferred_element_type=f32)
            step_send[...] = jnp.concatenate([steps, jnp.zeros((8, LANES - sp), f32)], axis=1)
            remote(step_send, step_recv, STEP, sibling).start()
        wait(bar_buf.at[t, others], recv_sems.at[BAR + t])
        if chips <= 32:
            whole = jnp.concatenate([bar_buf[t, m] for m in range(chips)], axis=1)
            product = lax.dot_general(whole, dense[...], NT, preferred_element_type=f32)
        else:
            product = fold(0, chips, lambda m, total: total + lax.dot_general(
                bar_buf[t, m], dense[:, block_at(m)], NT, preferred_element_type=f32),
                jnp.zeros((sp, 2 * LANES), f32))
        product = (product[:, :LANES], product[:, LANES:])
        swap_send[t, 0] = product[1]
        swap_send[t, 1] = product[0]
        remote(swap_send.at[t], swap_recv.at[t], SWAP + t, sibling).start()
        wait(swap_recv.at[t], recv_sems.at[SWAP + t])
        y = tuple(y[i] + dual_step * (need[i] - (product[i] + swap_recv[t, i])) for i in range(2))
        sum_y = tuple(sum_y[i] + y[i] for i in range(2))

    y_avg = tuple(total / ITERS for total in sum_y)
    y_out[0] = y_avg[0][:s]
    wait(step_recv, recv_sems.at[STEP])
    weights = (start_send[1, s:s + 1], start_recv[1, s:s + 1])
    areas = (start_send[1, s + 1:s + 2], start_recv[1, s + 1:s + 2])
    numbers = lax.broadcasted_iota(jnp.int32, (AREAS, LANES), 0).astype(f32)

    def by_core(pair):
        return jnp.concatenate([jnp.where(core == 0, pair[0], pair[1]),
                                jnp.where(core == 0, pair[1], pair[0])], axis=1)

    weighted = by_core([weights[i] * jnp.where(rows == s, 1.0, y_avg[i]) for i in range(2)])
    onehot = by_core([(numbers == areas[i]).astype(f32) for i in range(2)])
    sums = lax.dot_general(weighted, onehot, NT, precision=FULL, preferred_element_type=f32)
    squares = [(y_avg[i] - first_y[i]) ** 2 for i in range(2)]
    dual_steps = lax.dot_general(jnp.ones((8, LANES), f32), squares[0] + squares[1], NT,
                                 precision=FULL, preferred_element_type=f32)
    steps = jnp.concatenate([(step_send[...] + step_recv[...])[:, :sp], dual_steps], axis=1)
    sums = jnp.where(rows[:, :AREAS] == s + 1, steps[:1], sums)
    half = sp // 2
    last_send[...] = jnp.concatenate([sums[:half], sums[half:]], axis=1)
    each(1, chips, lambda d: remote(
        last_send, last_recv.at[chip], LAST, peer(chips - d)).start())
    last_recv[chip] = last_send[...]
    wait(last_recv.at[pl.ds(0, chips - 1)], recv_sems.at[LAST])
    total = fold(1, chips, lambda d, total: total + last_recv[d], last_recv[0])
    sums = jnp.concatenate([total[:, :AREAS], total[:, AREAS:]], axis=0)
    price = sums / sums[s:s + 1]
    price_out[...] = price.T[:, :s]
    ends = sums[s + 1:s + 2] + small_eps
    weight_out[...] = jnp.sqrt(ends[:, sp:sp + s] / ends[:, :s])

    for t in range(ITERS):
        wait(part_send.at[t, others], send_sems.at[PART + t])
        wait(bar_buf.at[t, others], send_sems.at[BAR + t])
        wait(swap_send.at[t], send_sems.at[SWAP + t])
    wait(start_send, send_sems.at[START])
    wait(stage, send_sems.at[MATRIX])
    wait(step_send, send_sems.at[STEP])
    wait(last_recv.at[pl.ds(0, chips - 1)], send_sems.at[LAST])


def per_device(n, tiles, column_ids, costs, upper, demand, x_start, y_start, row_weight, area):
    s = costs.shape[1]
    sp = -(-(s + 2) // 16) * 16
    chips = n // 2
    if n % 2 or chips & (chips - 1) or tiles.shape[0] != 1:
        raise ValueError("unsupported mesh")
    f32 = jnp.float32
    vmem = pl.BlockSpec(memory_space=pltpu.VMEM)
    anywhere = pl.BlockSpec(memory_space=pl.ANY)
    phases = 3 * ITERS + 4
    by_case = [jnp.transpose(a, (1, 0, 2)) for a in (costs, upper, demand, x_start, y_start)]
    x_avg, y_avg, price, weight = pl.pallas_call(
        functools.partial(kernel, n),
        out_shape=(
            jax.ShapeDtypeStruct(x_start.shape, f32),
            jax.ShapeDtypeStruct(y_start.shape, f32),
            jax.ShapeDtypeStruct((AREAS, s), f32),
            jax.ShapeDtypeStruct((1, s), f32),
        ),
        in_specs=[anywhere, pl.BlockSpec(memory_space=pltpu.SMEM)] + [anywhere] * 7,
        out_specs=[vmem] * 4,
        scratch_shapes=[
            pltpu.VMEM(tiles.shape[1:], jnp.bfloat16),
            pltpu.VMEM((5, sp, LANES), f32),
            pltpu.VMEM((2, 1, LANES), f32),
            pltpu.VMEM((2 * LANES, chips * LANES), jnp.bfloat16),
            pltpu.VMEM((LANES, chips * LANES), jnp.bfloat16),
            pltpu.VMEM((2, sp, LANES), f32),
            pltpu.VMEM((2, sp, LANES), f32),
            pltpu.VMEM((ITERS, chips, sp, LANES), f32),
            pltpu.VMEM((ITERS, chips, sp, LANES), f32),
            pltpu.VMEM((ITERS, chips, sp, LANES), jnp.bfloat16),
            pltpu.VMEM((ITERS, 2, sp, LANES), f32),
            pltpu.VMEM((ITERS, 2, sp, LANES), f32),
            pltpu.VMEM((8, LANES), f32),
            pltpu.VMEM((8, LANES), f32),
            pltpu.VMEM((sp // 2, LANES), f32),
            pltpu.VMEM((chips, sp // 2, LANES), f32),
            pltpu.SemaphoreType.DMA((8,)),
            pltpu.SemaphoreType.DMA((phases,)),
            pltpu.SemaphoreType.DMA((phases,)),
        ],
        compiler_params=pltpu.CompilerParams(
            collective_id=0, has_side_effects=True, vmem_limit_bytes=44 * 2**20
        ),
    )(tiles, column_ids, *by_case, row_weight, area.astype(f32).reshape(1, -1))
    return x_avg, y_avg, price, weight.reshape(s)


def solution(mesh):
    case = P(("groups", "rows"), None, None)
    in_specs = (
        P("rows", None, None, None), P("rows", None), case, case, case, case, case,
        P("rows", None), P("rows"),
    )
    out_specs = (case, case, P("groups", None), P("groups"))
    return jax.shard_map(
        functools.partial(per_device, mesh.shape["rows"]),
        mesh=mesh, in_specs=in_specs, out_specs=out_specs, check_vma=False,
    )
```

```python
import functools

import jax
import jax.numpy as jnp
from jax import lax
from jax.experimental import pallas as pl
from jax.experimental.pallas import tpu as pltpu
from jax.sharding import PartitionSpec as P

ITERS = 4
AREAS = 64
LANES = 128

primal_step = 0.3
dual_step = 0.3
small_eps = 1e-06

NT = (((1,), (1,)), ((), ()))

def split(value):
    parts = []
    for _ in range(3):
        parts.append(value.astype(jnp.bfloat16))
        value = value - parts[-1].astype(jnp.float32)
    return parts


def fold(lo, hi, body, carry):
    if hi - lo <= 32:
        for d in range(lo, hi):
            carry = body(d, carry)
        return carry
    return lax.fori_loop(lo, hi, body, carry)


def each(lo, hi, body):
    def step(d, carry):
        body(d)
        return carry

    fold(lo, hi, step, 0)


def block_at(d, width=LANES):
    start = d * width
    if not isinstance(start, int):
        start = pl.multiple_of(start, LANES)
    return pl.ds(start, width)


def flipped(number, mask, count):
    result, bit = 0, 1
    while bit < count:
        b = lax.rem(lax.div(number, bit), 2)
        if isinstance(mask, int):
            b = 1 - b if mask // bit % 2 else b
        else:
            m = lax.rem(lax.div(mask, bit), 2)
            b = b + m - 2 * b * m
        result = result + b * bit
        bit = 2 * bit
    return result


def kernel(
    n, tiles_in, ids_in, costs, upper, demand, x_start, y_start, row_weight, area,
    x_out, y_out, price_out, weight_out,
    tiles, ids, cases, weight_row, area_row, results, dense, turned, stage, start_send, start_recv, part_send, part_recv, bar_buf,
    swap_send, swap_recv, step_send, step_recv, last_send, last_recv,
    in_sems, send_sems, recv_sems,
):
    me = lax.axis_index("rows")
    core = lax.rem(me, 2)
    chip = lax.div(me, 2)
    chips = n // 2
    count = tiles_in.shape[1]
    s = costs.shape[0]
    sp = bar_buf.shape[2]
    f32 = jnp.float32
    sibling = {"rows": me + 1 - 2 * core}
    PART, NEAR, FAR, SWAP = (i * ITERS for i in range(4))
    START, MATRIX, STEP, LAST = (4 * ITERS + i for i in range(4))

    half = chips // 2
    near, far = pl.ds(1, half - 1), pl.ds(half, chips - half)

    def peer(m):
        return {"rows": 2 * flipped(chip, m, chips) + core}

    def remote(src, dst, phase, where):
        return pltpu.make_async_remote_copy(
            src_ref=src, dst_ref=dst, send_sem=send_sems.at[phase], recv_sem=recv_sems.at[phase],
            device_id=where, device_id_type=pl.DeviceIdType.MESH,
        )

    def wait(ref, sem):
        pltpu.make_async_copy(ref, ref, sem).wait()

    def signal(where):
        pl.semaphore_signal(barrier, inc=1, device_id=where, device_id_type=pl.DeviceIdType.MESH)

    barrier = pltpu.get_barrier_semaphore()
    loads = [pltpu.make_async_copy(tiles_in.at[0], tiles, in_sems.at[0])]
    for i, ref in enumerate((costs, upper, demand, x_start, y_start)):
        loads.append(pltpu.make_async_copy(
            ref.at[:, 0], cases.at[i, pl.ds(0, s)], in_sems.at[1 + i]))
    loads.append(pltpu.make_async_copy(row_weight, weight_row, in_sems.at[6]))
    loads.append(pltpu.make_async_copy(area, area_row, in_sems.at[7]))
    loads.append(pltpu.make_async_copy(ids_in, ids, in_sems.at[8]))
    for load in loads:
        load.start()
    each(1, chips, lambda d: signal(peer(chips - d)))
    signal(sibling)
    cases[:, s:] = jnp.zeros((5, sp - s, LANES), f32)

    def find(column):
        return fold(0, count, lambda k, found: jnp.where(ids[0, k] == column, k, found),
                    jnp.int32(-1))

    for load in loads:
        load.wait()
    cost, top, first_x = cases[0], cases[1], cases[3]
    start_send[0] = cases[2]
    start_send[1] = cases[4]
    start_send[1, s:s + 1] = weight_row[...]
    start_send[1, s + 1:s + 2] = area_row[...].astype(f32)

    def place(m):
        other = flipped(chip, m, chips)
        for target, number in ((dense, core), (stage, 1 - core)):
            found = find(2 * other + number)
            tile = tiles[jnp.maximum(found, 0)]
            target[0:LANES, block_at(m)] = jnp.where(found >= 0, tile, jnp.zeros_like(tile))

    each(0, chips, place)
    pl.semaphore_wait(barrier, chips)
    remote(stage, dense.at[pl.ds(LANES, LANES)], MATRIX, sibling).start()
    remote(start_send, start_recv, START, sibling).start()

    rows = lax.broadcasted_iota(jnp.int32, (sp, LANES), 0)
    real = rows < s
    x = first_x
    sum_x = jnp.zeros_like(x)
    wait(start_recv, recv_sems.at[START])
    need = (cases[2], start_recv[0])
    first_y = (cases[4], jnp.where(real, start_recv[1], 0.0))
    y = first_y
    sum_y = (jnp.zeros_like(x), jnp.zeros_like(x))
    wait(stage, recv_sems.at[MATRIX])

    weights = (start_send[1, s:s + 1], start_recv[1, s:s + 1])
    areas = (start_send[1, s + 1:s + 2], start_recv[1, s + 1:s + 2])
    numbers = lax.broadcasted_iota(jnp.int32, (AREAS, LANES), 0).astype(f32)

    def by_core(pair):
        return jnp.concatenate([jnp.where(core == 0, pair[0], pair[1]),
                                jnp.where(core == 0, pair[1], pair[0])], axis=1)

    onehot = by_core([(numbers == areas[i]).astype(f32) for i in range(2)]).astype(jnp.bfloat16)

    def row_of_sums(value):
        parts = jnp.concatenate(split(value), axis=1)
        return lax.dot_general(jnp.ones((8, 3 * LANES), jnp.bfloat16), parts, NT,
                               preferred_element_type=f32)

    for t in range(ITERS):
        y_round = jnp.concatenate(y, axis=1).astype(jnp.bfloat16)

        def send_part(i):
            pair = chips // 2 - 1 - i
            both = jnp.dot(y_round, dense[:, block_at(pair, 2 * LANES)],
                           preferred_element_type=f32)
            for m, value in ((2 * pair + 1, both[:, LANES:]), (2 * pair, both[:, :LANES])):
                part_send[t, m] = value
                remote(part_send.at[t, m], part_recv.at[t, m], PART + t, peer(m)).start()

        each(0, chips // 2 - 1, send_part)
        both = jnp.dot(y_round, dense[:, 0:2 * LANES], preferred_element_type=f32)
        part_send[t, 1] = both[:, LANES:]
        remote(part_send.at[t, 1], part_recv.at[t, 1], PART + t, peer(1)).start()
        if t == 0:
            def turn(m):
                block = dense[:, block_at(m)]
                turned[block_at(m), :] = jnp.concatenate(
                    [block[:LANES].T, block[LANES:].T], axis=1)

            each(0, chips, turn)
        others = pl.ds(1, chips - 1)
        wait(part_recv.at[t, others], recv_sems.at[PART + t])
        product = fold(1, chips, lambda m, total: total + part_recv[t, m], both[:, :LANES])
        x_next = jnp.clip(x - primal_step * (cost - product), 0.0, top)
        bar_buf[t, 0] = (2.0 * x_next - x).astype(jnp.bfloat16)
        each(half, chips, lambda d: remote(
            bar_buf.at[t, 0], bar_buf.at[t, chips + half - 1 - d], FAR + t,
            peer(chips + half - 1 - d)).start())
        each(1, half, lambda d: remote(
            bar_buf.at[t, 0], bar_buf.at[t, half - d], NEAR + t, peer(half - d)).start())
        x = x_next
        sum_x = sum_x + x
        if t == ITERS - 1:
            x_avg = sum_x / ITERS
            results[0] = x_avg
            x_done = pltpu.make_async_copy(
                results.at[0, pl.ds(0, s)], x_out.at[:, 0], in_sems.at[0])
            x_done.start()
            steps = row_of_sums((x_avg - first_x) ** 2)
            step_send[...] = jnp.concatenate([steps, jnp.zeros((8, LANES - sp), f32)], axis=1)
            remote(step_send, step_recv, STEP, sibling).start()

        def multiply(lo, hi):
            if hi - lo <= 32:
                some = jnp.concatenate([bar_buf[t, m] for m in range(lo, hi)], axis=1)
                return jnp.dot(some, turned[lo * LANES:hi * LANES, :],
                               preferred_element_type=f32)
            return fold(lo, hi, lambda m, total: total + jnp.dot(
                bar_buf[t, m], turned[block_at(m), :], preferred_element_type=f32),
                jnp.zeros((sp, 2 * LANES), f32))

        wait(bar_buf.at[t, near], recv_sems.at[NEAR + t])
        product = multiply(0, half)
        wait(bar_buf.at[t, far], recv_sems.at[FAR + t])
        product = product + multiply(half, chips)
        product = (product[:, :LANES], product[:, LANES:])
        swap_send[t, 0] = product[1]
        swap_send[t, 1] = product[0]
        remote(swap_send.at[t], swap_recv.at[t], SWAP + t, sibling).start()
        wait(swap_recv.at[t], recv_sems.at[SWAP + t])
        y = tuple(y[i] + dual_step * (need[i] - (product[i] + swap_recv[t, i])) for i in range(2))
        sum_y = tuple(sum_y[i] + y[i] for i in range(2))

    y_avg = tuple(total / ITERS for total in sum_y)
    results[1] = y_avg[0]
    y_done = pltpu.make_async_copy(results.at[1, pl.ds(0, s)], y_out.at[:, 0], in_sems.at[1])
    y_done.start()
    wait(step_recv, recv_sems.at[STEP])
    weighted = by_core([weights[i] * jnp.where(rows == s, 1.0, y_avg[i]) for i in range(2)])
    sums = lax.dot_general(jnp.concatenate(split(weighted), axis=0), onehot, NT,
                           preferred_element_type=f32)
    sums = sums[:sp] + (sums[sp:2 * sp] + sums[2 * sp:])
    squares = [(y_avg[i] - first_y[i]) ** 2 for i in range(2)]
    dual_steps = row_of_sums(squares[0] + squares[1])
    steps = jnp.concatenate([(step_send[...] + step_recv[...])[:, :sp], dual_steps], axis=1)
    sums = jnp.where(rows[:, :AREAS] == s + 1, steps[:1], sums)
    top_half = sp // 2
    last_send[...] = jnp.concatenate([sums[:top_half], sums[top_half:]], axis=1)
    each(1, chips, lambda d: remote(
        last_send, last_recv.at[chip], LAST, peer(chips - d)).start())
    last_recv[chip] = last_send[...]
    wait(last_recv.at[pl.ds(0, chips - 1)], recv_sems.at[LAST])
    total = fold(1, chips, lambda d, total: total + last_recv[d], last_recv[0])
    sums = jnp.concatenate([total[:, :AREAS], total[:, AREAS:]], axis=0)
    price = sums / sums[s:s + 1]
    price_out[...] = price[:s]
    ends = sums[s + 1:s + 2] + small_eps
    weight_out[...] = jnp.sqrt(ends[:, sp:sp + s] / ends[:, :s])

    for t in range(ITERS):
        wait(part_send.at[t, others], send_sems.at[PART + t])
        wait(bar_buf.at[t, near], send_sems.at[NEAR + t])
        wait(bar_buf.at[t, far], send_sems.at[FAR + t])
        wait(swap_send.at[t], send_sems.at[SWAP + t])
    wait(start_send, send_sems.at[START])
    wait(stage, send_sems.at[MATRIX])
    wait(step_send, send_sems.at[STEP])
    wait(last_recv.at[pl.ds(0, chips - 1)], send_sems.at[LAST])
    x_done.wait()
    y_done.wait()


def hand_on(*refs):
    count = len(refs) // 2
    sems = refs[-1]
    copies = [pltpu.make_async_copy(refs[i], refs[count + i], sems.at[i]) for i in range(count)]
    for copy in copies:
        copy.start()
    for copy in copies:
        copy.wait()


def per_device(n, tiles, column_ids, costs, upper, demand, x_start, y_start, row_weight, area):
    s = costs.shape[1]
    sp = -(-(s + 2) // 16) * 16
    chips = n // 2
    if n % 2 or chips & (chips - 1) or chips < 4 or tiles.shape[0] != 1:
        raise ValueError("unsupported mesh")
    f32 = jnp.float32
    vmem = pl.BlockSpec(memory_space=pltpu.VMEM)
    anywhere = pl.BlockSpec(memory_space=pltpu.HBM)
    phases = 4 * ITERS + 4
    by_case = [jnp.transpose(a, (1, 0, 2)) for a in (costs, upper, demand, x_start, y_start)]
    results = pl.pallas_call(
        functools.partial(kernel, n),
        out_shape=(
            jax.ShapeDtypeStruct((s, 1, LANES), f32),
            jax.ShapeDtypeStruct((s, 1, LANES), f32),
            jax.ShapeDtypeStruct((s, AREAS), f32),
            jax.ShapeDtypeStruct((1, s), f32),
        ),
        in_specs=[anywhere] * 9,
        out_specs=[anywhere] * 2 + [vmem] * 2,
        scratch_shapes=[
            pltpu.VMEM(tiles.shape[1:], jnp.bfloat16),
            pltpu.SMEM(column_ids.shape, jnp.int32),
            pltpu.VMEM((5, sp, LANES), f32),
            pltpu.VMEM((1, LANES), f32),
            pltpu.VMEM((1, LANES), jnp.int32),
            pltpu.VMEM((2, sp, LANES), f32),
            pltpu.VMEM((2 * LANES, chips * LANES), jnp.bfloat16),
            pltpu.VMEM((chips * LANES, 2 * LANES), jnp.bfloat16),
            pltpu.VMEM((LANES, chips * LANES), jnp.bfloat16),
            pltpu.VMEM((2, sp, LANES), f32),
            pltpu.VMEM((2, sp, LANES), f32),
            pltpu.VMEM((ITERS, chips, sp, LANES), f32),
            pltpu.VMEM((ITERS, chips, sp, LANES), f32),
            pltpu.VMEM((ITERS, chips, sp, LANES), jnp.bfloat16),
            pltpu.VMEM((ITERS, 2, sp, LANES), f32),
            pltpu.VMEM((ITERS, 2, sp, LANES), f32),
            pltpu.VMEM((8, LANES), f32),
            pltpu.VMEM((8, LANES), f32),
            pltpu.VMEM((sp // 2, LANES), f32),
            pltpu.VMEM((chips, sp // 2, LANES), f32),
            pltpu.SemaphoreType.DMA((9,)),
            pltpu.SemaphoreType.DMA((phases,)),
            pltpu.SemaphoreType.DMA((phases,)),
        ],
        compiler_params=pltpu.CompilerParams(
            collective_id=0, has_side_effects=True, vmem_limit_bytes=60 * 2**20
        ),
    )(tiles, column_ids, *by_case, row_weight, area.reshape(1, -1))
    x_avg, y_avg, price, weight = pl.pallas_call(
        hand_on,
        out_shape=tuple(jax.ShapeDtypeStruct(a.shape, a.dtype) for a in results),
        in_specs=[anywhere] * 4,
        out_specs=[anywhere] * 4,
        scratch_shapes=[pltpu.SemaphoreType.DMA((4,))],
        compiler_params=pltpu.CompilerParams(vmem_limit_bytes=60 * 2**20),
    )(*results)
    x_avg, y_avg = (jnp.transpose(a, (1, 0, 2)) for a in (x_avg, y_avg))
    return x_avg, y_avg, price.T, weight.reshape(s)


def solution(mesh):
    case = P(("groups", "rows"), None, None)
    in_specs = (
        P("rows", None, None, None), P("rows", None), case, case, case, case, case,
        P("rows", None), P("rows"),
    )
    out_specs = (case, case, P("groups", None), P("groups"))
    return jax.shard_map(
        functools.partial(per_device, mesh.shape["rows"]),
        mesh=mesh, in_specs=in_specs, out_specs=out_specs, check_vma=False,
    )
```

```python
import functools

import jax
import jax.numpy as jnp
from jax import lax
from jax.experimental import pallas as pl
from jax.experimental.pallas import tpu as pltpu
from jax.sharding import PartitionSpec as P

ITERS = 4
AREAS = 64
LANES = 128

primal_step = 0.3
dual_step = 0.3
small_eps = 1e-06

NT = (((1,), (1,)), ((), ()))

def split(value):
    parts = []
    for _ in range(3):
        parts.append(value.astype(jnp.bfloat16))
        value = value - parts[-1].astype(jnp.float32)
    return parts


def fold(lo, hi, body, carry):
    if hi - lo <= 32:
        for d in range(lo, hi):
            carry = body(d, carry)
        return carry
    return lax.fori_loop(lo, hi, body, carry)


def each(lo, hi, body):
    def step(d, carry):
        body(d)
        return carry

    fold(lo, hi, step, 0)


def block_at(d, width=LANES):
    start = d * width
    if not isinstance(start, int):
        start = pl.multiple_of(start, LANES)
    return pl.ds(start, width)


def flipped(number, mask, count):
    result, bit = 0, 1
    while bit < count:
        b = lax.rem(lax.div(number, bit), 2)
        if isinstance(mask, int):
            b = 1 - b if mask // bit % 2 else b
        else:
            m = lax.rem(lax.div(mask, bit), 2)
            b = b + m - 2 * b * m
        result = result + b * bit
        bit = 2 * bit
    return result


def kernel(
    n, tiles_in, ids_in, costs, upper, demand, x_start, y_start, row_weight, area,
    x_out, y_out, price_out, weight_out,
    tiles, ids, cases, weight_row, area_row, results, dense, turned, stage, start_send, start_recv, part_send, part_recv, bar_buf,
    swap_send, swap_recv, step_send, step_recv, last_send, last_recv,
    in_sems, send_sems, recv_sems,
):
    me = lax.axis_index("rows")
    core = lax.rem(me, 2)
    chip = lax.div(me, 2)
    chips = n // 2
    count = tiles_in.shape[1]
    s = costs.shape[0]
    hp = bar_buf.shape[3]
    sp = 2 * hp
    f32 = jnp.float32
    sibling = {"rows": me + 1 - 2 * core}
    both = range(2)
    part_sem, near_sem, far_sem, swap_sem = (
        lambda t, h, kind=kind: (kind * ITERS + t) * 2 + h for kind in range(4))
    START, MATRIX, STEP, LAST = (8 * ITERS + i for i in range(4))

    half = chips // 2
    near, far = pl.ds(1, half - 1), pl.ds(half, chips - half)

    def far_chip(m):
        return 2 * flipped(chip, m, chips) + core

    known = [far_chip(m) for m in range(chips)] if chips <= 32 else None

    def peer(m):
        return {"rows": known[m] if known else far_chip(m)}

    def remote(src, dst, phase, where):
        return pltpu.make_async_remote_copy(
            src_ref=src, dst_ref=dst, send_sem=send_sems.at[phase], recv_sem=recv_sems.at[phase],
            device_id=where, device_id_type=pl.DeviceIdType.MESH,
        )

    def wait(ref, sem):
        pltpu.make_async_copy(ref, ref, sem).wait()

    def signal(where):
        pl.semaphore_signal(barrier, inc=1, device_id=where, device_id_type=pl.DeviceIdType.MESH)

    barrier = pltpu.get_barrier_semaphore()
    loads = [pltpu.make_async_copy(tiles_in.at[0], tiles, in_sems.at[0])]
    for i, ref in enumerate((costs, upper, demand, x_start, y_start)):
        loads.append(pltpu.make_async_copy(
            ref.at[:, 0], cases.at[i, pl.ds(0, s)], in_sems.at[1 + i]))
    loads.append(pltpu.make_async_copy(row_weight, weight_row, in_sems.at[6]))
    loads.append(pltpu.make_async_copy(area, area_row, in_sems.at[7]))
    loads.append(pltpu.make_async_copy(ids_in, ids, in_sems.at[8]))
    for load in loads:
        load.start()
    each(1, chips, lambda d: signal(peer(chips - d)))
    signal(sibling)
    cases[:, s:] = jnp.zeros((5, sp - s, LANES), f32)

    def find(column):
        return fold(0, count, lambda k, found: jnp.where(ids[0, k] == column, k, found),
                    jnp.int32(-1))

    for load in loads:
        load.wait()
    cost, top, first_x = cases[0], cases[1], cases[3]
    start_send[0] = cases[2]
    start_send[1] = cases[4]
    start_send[1, s:s + 1] = weight_row[...]
    start_send[1, s + 1:s + 2] = area_row[...].astype(f32)

    def place(m):
        other = flipped(chip, m, chips)
        for target, number in ((dense, core), (stage, 1 - core)):
            found = find(2 * other + number)
            tile = tiles[jnp.maximum(found, 0)]
            target[0:LANES, block_at(m)] = jnp.where(found >= 0, tile, jnp.zeros_like(tile))

    each(0, chips, place)
    pl.semaphore_wait(barrier, chips)
    remote(stage, dense.at[pl.ds(LANES, LANES)], MATRIX, sibling).start()
    remote(start_send, start_recv, START, sibling).start()

    rows = lax.broadcasted_iota(jnp.int32, (sp, LANES), 0)
    real = rows < s
    x = first_x
    sum_x = jnp.zeros_like(x)
    wait(start_recv, recv_sems.at[START])
    need = (cases[2], start_recv[0])
    first_y = (cases[4], jnp.where(real, start_recv[1], 0.0))

    def halves(value):
        return [value[h * hp:(h + 1) * hp] for h in both]

    cost, top, x = halves(cost), halves(top), halves(x)
    y = list(zip(halves(first_y[0]), halves(first_y[1])))
    need = list(zip(halves(need[0]), halves(need[1])))
    sum_x = halves(sum_x)
    sum_y = [(jnp.zeros_like(x[0]), jnp.zeros_like(x[0])) for h in both]
    wait(stage, recv_sems.at[MATRIX])

    weights = (start_send[1, s:s + 1], start_recv[1, s:s + 1])
    areas = (start_send[1, s + 1:s + 2], start_recv[1, s + 1:s + 2])
    numbers = lax.broadcasted_iota(jnp.int32, (AREAS, LANES), 0).astype(f32)

    def by_core(pair):
        return jnp.concatenate([jnp.where(core == 0, pair[0], pair[1]),
                                jnp.where(core == 0, pair[1], pair[0])], axis=1)

    onehot = by_core([(numbers == areas[i]).astype(f32) for i in range(2)]).astype(jnp.bfloat16)

    def row_of_sums(value):
        parts = jnp.concatenate(split(value), axis=1)
        return lax.dot_general(jnp.ones((8, 3 * LANES), jnp.bfloat16), parts, NT,
                               preferred_element_type=f32)

    others = pl.ds(1, chips - 1)
    for t in range(ITERS):
        first = [None, None]
        for h in both:
            y_round = jnp.concatenate(y[h], axis=1).astype(jnp.bfloat16)

            def send_part(i, h=h, y_round=y_round):
                pair = chips // 2 - 1 - i
                two = jnp.dot(y_round, dense[:, block_at(pair, 2 * LANES)],
                              preferred_element_type=f32)
                part_send[t, h, 2 * pair + 1] = two[:, LANES:]
                part_send[t, h, 2 * pair] = two[:, :LANES]
                for m in (2 * pair + 1, 2 * pair):
                    remote(part_send.at[t, h, m], part_recv.at[t, h, m], part_sem(t, h),
                           peer(m)).start()

            each(0, chips // 2 - 1, send_part)
            two = jnp.dot(y_round, dense[:, 0:2 * LANES], preferred_element_type=f32)
            part_send[t, h, 1] = two[:, LANES:]
            remote(part_send.at[t, h, 1], part_recv.at[t, h, 1], part_sem(t, h), peer(1)).start()
            first[h] = two[:, :LANES]
        if t == 0:
            def turn(m):
                block = dense[:, block_at(m)]
                turned[block_at(m), :] = jnp.concatenate(
                    [block[:LANES].T, block[LANES:].T], axis=1)

            each(0, chips, turn)
        for h in both:
            wait(part_recv.at[t, h, others], recv_sems.at[part_sem(t, h)])
            product = fold(1, chips, lambda m, total: total + part_recv[t, h, m], first[h])
            x_next = jnp.clip(x[h] - primal_step * (cost[h] - product), 0.0, top[h])
            bar_buf[t, h, 0] = (2.0 * x_next - x[h]).astype(jnp.bfloat16)

            def send_bar(m, sem, h=h):
                remote(bar_buf.at[t, h, 0], bar_buf.at[t, h, m], sem, peer(m)).start()

            each(half, chips, lambda d: send_bar(chips + half - 1 - d, near_sem(t, h)))
            each(1, half, lambda d: send_bar(half - d, near_sem(t, h)))
            x[h] = x_next
            sum_x[h] = sum_x[h] + x_next
        if t == ITERS - 1:
            x_avg = jnp.concatenate(sum_x, axis=0) / ITERS
            results[0] = x_avg
            x_done = pltpu.make_async_copy(
                results.at[0, pl.ds(0, s)], x_out.at[:, 0], in_sems.at[0])
            x_done.start()
            steps = row_of_sums((x_avg - first_x) ** 2)
            step_send[...] = jnp.concatenate([steps, jnp.zeros((8, LANES - sp), f32)], axis=1)
            remote(step_send, step_recv, STEP, sibling).start()

        def multiply(lo, hi, which):
            def arrived(m):
                return jnp.concatenate([bar_buf[t, h, m] for h in which], axis=0)

            if hi - lo <= 32:
                some = jnp.concatenate([arrived(m) for m in range(lo, hi)], axis=1)
                return jnp.dot(some, turned[lo * LANES:hi * LANES, :],
                               preferred_element_type=f32)
            return fold(lo, hi, lambda m, total: total + jnp.dot(
                arrived(m), turned[block_at(m), :], preferred_element_type=f32),
                jnp.zeros((len(which) * hp, 2 * LANES), f32))

        products = [None, None]
        for h in both:
            wait(bar_buf.at[t, h, others], recv_sems.at[near_sem(t, h)])
            product = multiply(0, chips, (h,))
            products[h] = (product[:, :LANES], product[:, LANES:])
            swap_send[t, h, 0] = products[h][1]
            swap_send[t, h, 1] = products[h][0]
            remote(swap_send.at[t, h], swap_recv.at[t, h], swap_sem(t, h), sibling).start()
        for h in both:
            wait(swap_recv.at[t, h], recv_sems.at[swap_sem(t, h)])
            y[h] = tuple(
                y[h][i] + dual_step * (need[h][i] - (products[h][i] + swap_recv[t, h, i]))
                for i in range(2))
            sum_y[h] = tuple(sum_y[h][i] + y[h][i] for i in range(2))

    y_avg = tuple(
        jnp.concatenate([sum_y[h][i] for h in both], axis=0) / ITERS for i in range(2))
    results[1] = y_avg[0]
    y_done = pltpu.make_async_copy(results.at[1, pl.ds(0, s)], y_out.at[:, 0], in_sems.at[1])
    y_done.start()
    wait(step_recv, recv_sems.at[STEP])
    weighted = by_core([weights[i] * jnp.where(rows == s, 1.0, y_avg[i]) for i in range(2)])
    sums = lax.dot_general(jnp.concatenate(split(weighted), axis=0), onehot, NT,
                           preferred_element_type=f32)
    sums = sums[:sp] + (sums[sp:2 * sp] + sums[2 * sp:])
    squares = [(y_avg[i] - first_y[i]) ** 2 for i in range(2)]
    dual_steps = row_of_sums(squares[0] + squares[1])
    steps = jnp.concatenate([(step_send[...] + step_recv[...])[:, :sp], dual_steps], axis=1)
    sums = jnp.where(rows[:, :AREAS] == s + 1, steps[:1], sums)
    top_half = sp // 2
    last_send[...] = jnp.concatenate([sums[:top_half], sums[top_half:]], axis=1)
    each(1, chips, lambda d: remote(
        last_send, last_recv.at[chip], LAST, peer(chips - d)).start())
    last_recv[chip] = last_send[...]
    wait(last_recv.at[pl.ds(0, chips - 1)], recv_sems.at[LAST])
    total = fold(1, chips, lambda d, total: total + last_recv[d], last_recv[0])
    sums = jnp.concatenate([total[:, :AREAS], total[:, AREAS:]], axis=0)
    price = sums / sums[s:s + 1]
    price_out[...] = price[:s]
    ends = sums[s + 1:s + 2] + small_eps
    weight_out[...] = jnp.sqrt(ends[:, sp:sp + s] / ends[:, :s])

    for t in range(ITERS):
        for h in both:
            wait(part_send.at[t, h, others], send_sems.at[part_sem(t, h)])
            wait(bar_buf.at[t, h, others], send_sems.at[near_sem(t, h)])
            wait(swap_send.at[t, h], send_sems.at[swap_sem(t, h)])
    wait(start_send, send_sems.at[START])
    wait(stage, send_sems.at[MATRIX])
    wait(step_send, send_sems.at[STEP])
    wait(last_recv.at[pl.ds(0, chips - 1)], send_sems.at[LAST])
    x_done.wait()
    y_done.wait()


def hand_on(*refs):
    count = len(refs) // 2
    for i in range(count):
        refs[count + i][...] = refs[i][...]


def per_device(n, tiles, column_ids, costs, upper, demand, x_start, y_start, row_weight, area):
    s = costs.shape[1]
    hp = -(-(s + 2) // 32) * 16
    sp = 2 * hp
    chips = n // 2
    if n % 2 or chips & (chips - 1) or chips < 4 or tiles.shape[0] != 1:
        raise ValueError("unsupported mesh")
    f32 = jnp.float32
    vmem = pl.BlockSpec(memory_space=pltpu.VMEM)
    anywhere = pl.BlockSpec(memory_space=pltpu.HBM)
    phases = 8 * ITERS + 4
    by_case = [jnp.transpose(a, (1, 0, 2)) for a in (costs, upper, demand, x_start, y_start)]
    results = pl.pallas_call(
        functools.partial(kernel, n),
        out_shape=(
            jax.ShapeDtypeStruct((s, 1, LANES), f32),
            jax.ShapeDtypeStruct((s, 1, LANES), f32),
            jax.ShapeDtypeStruct((s, AREAS), f32),
            jax.ShapeDtypeStruct((1, s), f32),
        ),
        in_specs=[anywhere] * 9,
        out_specs=[anywhere] * 2 + [vmem] * 2,
        scratch_shapes=[
            pltpu.VMEM(tiles.shape[1:], jnp.bfloat16),
            pltpu.SMEM(column_ids.shape, jnp.int32),
            pltpu.VMEM((5, sp, LANES), f32),
            pltpu.VMEM((1, LANES), f32),
            pltpu.VMEM((1, LANES), jnp.int32),
            pltpu.VMEM((2, sp, LANES), f32),
            pltpu.VMEM((2 * LANES, chips * LANES), jnp.bfloat16),
            pltpu.VMEM((chips * LANES, 2 * LANES), jnp.bfloat16),
            pltpu.VMEM((LANES, chips * LANES), jnp.bfloat16),
            pltpu.VMEM((2, sp, LANES), f32),
            pltpu.VMEM((2, sp, LANES), f32),
            pltpu.VMEM((ITERS, 2, chips, hp, LANES), f32),
            pltpu.VMEM((ITERS, 2, chips, hp, LANES), f32),
            pltpu.VMEM((ITERS, 2, chips, hp, LANES), jnp.bfloat16),
            pltpu.VMEM((ITERS, 2, 2, hp, LANES), f32),
            pltpu.VMEM((ITERS, 2, 2, hp, LANES), f32),
            pltpu.VMEM((8, LANES), f32),
            pltpu.VMEM((8, LANES), f32),
            pltpu.VMEM((sp // 2, LANES), f32),
            pltpu.VMEM((chips, sp // 2, LANES), f32),
            pltpu.SemaphoreType.DMA((9,)),
            pltpu.SemaphoreType.DMA((phases,)),
            pltpu.SemaphoreType.DMA((phases,)),
        ],
        compiler_params=pltpu.CompilerParams(
            collective_id=0, has_side_effects=True, vmem_limit_bytes=60 * 2**20
        ),
    )(tiles, column_ids, *by_case, row_weight, area.reshape(1, -1))
    x_avg, y_avg, price, weight = pl.pallas_call(
        hand_on,
        out_shape=tuple(jax.ShapeDtypeStruct(a.shape, a.dtype) for a in results),
        in_specs=[vmem] * 4,
        out_specs=[vmem] * 4,
        compiler_params=pltpu.CompilerParams(vmem_limit_bytes=60 * 2**20),
    )(*results)
    x_avg, y_avg = (jnp.transpose(a, (1, 0, 2)) for a in (x_avg, y_avg))
    return x_avg, y_avg, price.T, weight.reshape(s)


def solution(mesh):
    case = P(("groups", "rows"), None, None)
    in_specs = (
        P("rows", None, None, None), P("rows", None), case, case, case, case, case,
        P("rows", None), P("rows"),
    )
    out_specs = (case, case, P("groups", None), P("groups"))
    return jax.shard_map(
        functools.partial(per_device, mesh.shape["rows"]),
        mesh=mesh, in_specs=in_specs, out_specs=out_specs, check_vma=False,
    )
```

```python
import functools

import jax
import jax.numpy as jnp
from jax import lax
from jax.experimental import pallas as pl
from jax.experimental.pallas import tpu as pltpu
from jax.sharding import PartitionSpec as P

ITERS = 4
AREAS = 64
LANES = 128

primal_step = 0.3
dual_step = 0.3
small_eps = 1e-06

NT = (((1,), (1,)), ((), ()))

def split(value):
    parts = []
    for _ in range(3):
        parts.append(value.astype(jnp.bfloat16))
        value = value - parts[-1].astype(jnp.float32)
    return parts


def fold(lo, hi, body, carry):
    if hi - lo <= 32:
        for d in range(lo, hi):
            carry = body(d, carry)
        return carry
    return lax.fori_loop(lo, hi, body, carry)


def each(lo, hi, body):
    def step(d, carry):
        body(d)
        return carry

    fold(lo, hi, step, 0)


def block_at(d, width=LANES):
    start = d * width
    if not isinstance(start, int):
        start = pl.multiple_of(start, LANES)
    return pl.ds(start, width)


def flipped(number, mask, count):
    result, bit = 0, 1
    while bit < count:
        b = lax.rem(lax.div(number, bit), 2)
        if isinstance(mask, int):
            b = 1 - b if mask // bit % 2 else b
        else:
            m = lax.rem(lax.div(mask, bit), 2)
            b = b + m - 2 * b * m
        result = result + b * bit
        bit = 2 * bit
    return result


def kernel(
    n, tiles_in, ids_in, costs, upper, demand, x_start, y_start, row_weight, area,
    x_out, y_out, price_out, weight_out,
    tiles, ids, cases, weight_row, area_row, results, dense, turned, stage, start_send, start_recv, part_send, part_recv, bar_buf,
    early_send, early_recv, swap_send, swap_recv, step_send, step_recv, last_send, last_recv,
    in_sems, send_sems, recv_sems,
):
    me = lax.axis_index("rows")
    core = lax.rem(me, 2)
    chip = lax.div(me, 2)
    chips = n // 2
    count = tiles_in.shape[1]
    s = costs.shape[0]
    hp = bar_buf.shape[3]
    sp = 2 * hp
    f32 = jnp.float32
    sibling = {"rows": me + 1 - 2 * core}
    both = range(2)
    part_sem, near_sem, far_sem, swap_sem = (
        lambda t, h, kind=kind: (kind * ITERS + t) * 2 + h for kind in range(4))
    START, MATRIX, STEP, LAST, EARLY = (8 * ITERS + i for i in range(5))

    half = chips // 2
    near, far = pl.ds(1, half - 1), pl.ds(half, chips - half)

    def far_chip(m):
        return 2 * flipped(chip, m, chips) + core

    known = [far_chip(m) for m in range(chips)] if chips <= 32 else None

    def peer(m):
        return {"rows": known[m] if known else far_chip(m)}

    def remote(src, dst, phase, where):
        return pltpu.make_async_remote_copy(
            src_ref=src, dst_ref=dst, send_sem=send_sems.at[phase], recv_sem=recv_sems.at[phase],
            device_id=where, device_id_type=pl.DeviceIdType.MESH,
        )

    def wait(ref, sem):
        pltpu.make_async_copy(ref, ref, sem).wait()

    def signal(where):
        pl.semaphore_signal(barrier, inc=1, device_id=where, device_id_type=pl.DeviceIdType.MESH)

    barrier = pltpu.get_barrier_semaphore()
    each(1, chips, lambda d: signal(peer(chips - d)))
    signal(sibling)
    loads = [pltpu.make_async_copy(tiles_in.at[0], tiles, in_sems.at[0])]
    for i, ref in enumerate((costs, upper, demand, x_start, y_start)):
        loads.append(pltpu.make_async_copy(
            ref.at[:, 0], cases.at[i, pl.ds(0, s)], in_sems.at[1 + i]))
    loads.append(pltpu.make_async_copy(row_weight, weight_row, in_sems.at[6]))
    loads.append(pltpu.make_async_copy(area, area_row, in_sems.at[7]))
    loads.append(pltpu.make_async_copy(ids_in, ids, in_sems.at[8]))
    for load in loads:
        load.start()
    cases[:, s:] = jnp.zeros((5, sp - s, LANES), f32)

    def find(column):
        return fold(0, count, lambda k, found: jnp.where(ids[0, k] == column, k, found),
                    jnp.int32(-1))

    for load in loads:
        load.wait()
    cost, top, first_x = cases[0], cases[1], cases[3]
    start_send[0] = cases[2]
    start_send[1] = cases[4]
    start_send[1, s:s + 1] = weight_row[...]
    start_send[1, s + 1:s + 2] = area_row[...].astype(f32)

    def place(m):
        other = flipped(chip, m, chips)
        for target, number in ((dense, core), (stage, 1 - core)):
            found = find(2 * other + number)
            tile = tiles[jnp.maximum(found, 0)]
            target[0:LANES, block_at(m)] = jnp.where(found >= 0, tile, jnp.zeros_like(tile))

    each(0, chips, place)
    rounded = cases[4].astype(jnp.bfloat16)

    def early(m):
        for target, matrix in ((part_send.at[0], dense), (early_send, stage)):
            value = jnp.dot(rounded, matrix[0:LANES, block_at(m)], preferred_element_type=f32)
            for h in both:
                target[h, m] = value[h * hp:(h + 1) * hp]

    each(0, chips, early)
    pl.semaphore_wait(barrier, chips)
    remote(early_send, early_recv, EARLY, sibling).start()
    remote(start_send, start_recv, START, sibling).start()

    rows = lax.broadcasted_iota(jnp.int32, (sp, LANES), 0)
    real = rows < s
    x = first_x
    sum_x = jnp.zeros_like(x)
    wait(early_recv, recv_sems.at[EARLY])
    for h in both:
        def send_early(d, h=h):
            m = chips - d
            part_send[0, h, m] = part_send[0, h, m] + early_recv[h, m]
            remote(part_send.at[0, h, m], part_recv.at[0, h, m], part_sem(0, h), peer(m)).start()

        each(1, chips, send_early)
    first = [part_send[0, h, 0] + early_recv[h, 0] for h in both]
    remote(stage, dense.at[pl.ds(LANES, LANES)], MATRIX, sibling).start()
    wait(start_recv, recv_sems.at[START])
    need = (cases[2], start_recv[0])
    first_y = (cases[4], jnp.where(real, start_recv[1], 0.0))

    def halves(value):
        return [value[h * hp:(h + 1) * hp] for h in both]

    cost, top, x = halves(cost), halves(top), halves(x)
    y = list(zip(halves(first_y[0]), halves(first_y[1])))
    need = list(zip(halves(need[0]), halves(need[1])))
    sum_x = halves(sum_x)
    sum_y = [(jnp.zeros_like(x[0]), jnp.zeros_like(x[0])) for h in both]
    wait(stage, recv_sems.at[MATRIX])

    weights = (start_send[1, s:s + 1], start_recv[1, s:s + 1])
    areas = (start_send[1, s + 1:s + 2], start_recv[1, s + 1:s + 2])
    numbers = lax.broadcasted_iota(jnp.int32, (AREAS, LANES), 0).astype(f32)

    def by_core(pair):
        return jnp.concatenate([jnp.where(core == 0, pair[0], pair[1]),
                                jnp.where(core == 0, pair[1], pair[0])], axis=1)

    onehot = by_core([(numbers == areas[i]).astype(f32) for i in range(2)]).astype(jnp.bfloat16)

    def row_of_sums(value):
        parts = jnp.concatenate(split(value), axis=1)
        return lax.dot_general(jnp.ones((8, 3 * LANES), jnp.bfloat16), parts, NT,
                               preferred_element_type=f32)

    others = pl.ds(1, chips - 1)
    for t in range(ITERS):
        if t > 0:
            first = [None, None]
            for h in both:
                y_round = jnp.concatenate(y[h], axis=1).astype(jnp.bfloat16)

                def send_part(i, h=h, y_round=y_round):
                    pair = chips // 2 - 1 - i
                    two = jnp.dot(y_round, dense[:, block_at(pair, 2 * LANES)],
                                  preferred_element_type=f32)
                    part_send[t, h, 2 * pair + 1] = two[:, LANES:]
                    part_send[t, h, 2 * pair] = two[:, :LANES]
                    for m in (2 * pair + 1, 2 * pair):
                        remote(part_send.at[t, h, m], part_recv.at[t, h, m], part_sem(t, h),
                               peer(m)).start()

                each(0, chips // 2 - 1, send_part)
                two = jnp.dot(y_round, dense[:, 0:2 * LANES], preferred_element_type=f32)
                part_send[t, h, 1] = two[:, LANES:]
                remote(part_send.at[t, h, 1], part_recv.at[t, h, 1], part_sem(t, h), peer(1)).start()
                first[h] = two[:, :LANES]
        if t == 0:
            def turn(m):
                block = dense[:, block_at(m)]
                turned[block_at(m), :] = jnp.concatenate(
                    [block[:LANES].T, block[LANES:].T], axis=1)

            each(0, chips, turn)
        for h in both:
            wait(part_recv.at[t, h, others], recv_sems.at[part_sem(t, h)])
            product = fold(1, chips, lambda m, total: total + part_recv[t, h, m], first[h])
            x_next = jnp.clip(x[h] - primal_step * (cost[h] - product), 0.0, top[h])
            bar_buf[t, h, 0] = (2.0 * x_next - x[h]).astype(jnp.bfloat16)

            def send_bar(m, sem, h=h):
                remote(bar_buf.at[t, h, 0], bar_buf.at[t, h, m], sem, peer(m)).start()

            each(half, chips, lambda d: send_bar(chips + half - 1 - d, near_sem(t, h)))
            each(1, half, lambda d: send_bar(half - d, near_sem(t, h)))
            x[h] = x_next
            sum_x[h] = sum_x[h] + x_next
        if t == ITERS - 1:
            x_avg = jnp.concatenate(sum_x, axis=0) / ITERS
            results[0] = x_avg
            x_done = pltpu.make_async_copy(
                results.at[0, pl.ds(0, s)], x_out.at[:, 0], in_sems.at[0])
            x_done.start()
            steps = row_of_sums((x_avg - first_x) ** 2)
            step_send[...] = jnp.concatenate([steps, jnp.zeros((8, LANES - sp), f32)], axis=1)
            remote(step_send, step_recv, STEP, sibling).start()

        def multiply(lo, hi, which):
            def arrived(m):
                return jnp.concatenate([bar_buf[t, h, m] for h in which], axis=0)

            if hi - lo <= 32:
                some = jnp.concatenate([arrived(m) for m in range(lo, hi)], axis=1)
                return jnp.dot(some, turned[lo * LANES:hi * LANES, :],
                               preferred_element_type=f32)
            return fold(lo, hi, lambda m, total: total + jnp.dot(
                arrived(m), turned[block_at(m), :], preferred_element_type=f32),
                jnp.zeros((len(which) * hp, 2 * LANES), f32))

        products = [None, None]
        for h in both:
            wait(bar_buf.at[t, h, others], recv_sems.at[near_sem(t, h)])
            product = multiply(0, chips, (h,))
            products[h] = (product[:, :LANES], product[:, LANES:])
            swap_send[t, h, 0] = products[h][1]
            swap_send[t, h, 1] = products[h][0]
            remote(swap_send.at[t, h], swap_recv.at[t, h], swap_sem(t, h), sibling).start()
        for h in both:
            wait(swap_recv.at[t, h], recv_sems.at[swap_sem(t, h)])
            y[h] = tuple(
                y[h][i] + dual_step * (need[h][i] - (products[h][i] + swap_recv[t, h, i]))
                for i in range(2))
            sum_y[h] = tuple(sum_y[h][i] + y[h][i] for i in range(2))

    y_avg = tuple(
        jnp.concatenate([sum_y[h][i] for h in both], axis=0) / ITERS for i in range(2))
    results[1] = y_avg[0]
    y_done = pltpu.make_async_copy(results.at[1, pl.ds(0, s)], y_out.at[:, 0], in_sems.at[1])
    y_done.start()
    wait(step_recv, recv_sems.at[STEP])
    weighted = by_core([weights[i] * jnp.where(rows == s, 1.0, y_avg[i]) for i in range(2)])
    sums = lax.dot_general(jnp.concatenate(split(weighted), axis=0), onehot, NT,
                           preferred_element_type=f32)
    sums = sums[:sp] + (sums[sp:2 * sp] + sums[2 * sp:])
    squares = [(y_avg[i] - first_y[i]) ** 2 for i in range(2)]
    dual_steps = row_of_sums(squares[0] + squares[1])
    steps = jnp.concatenate([(step_send[...] + step_recv[...])[:, :sp], dual_steps], axis=1)
    sums = jnp.where(rows[:, :AREAS] == s + 1, steps[:1], sums)
    top_half = sp // 2
    last_send[...] = jnp.concatenate([sums[:top_half], sums[top_half:]], axis=1)
    each(1, chips, lambda d: remote(
        last_send, last_recv.at[chip], LAST, peer(chips - d)).start())
    last_recv[chip] = last_send[...]
    for t in range(ITERS):
        for h in both:
            wait(part_send.at[t, h, others], send_sems.at[part_sem(t, h)])
            wait(bar_buf.at[t, h, others], send_sems.at[near_sem(t, h)])
            wait(swap_send.at[t, h], send_sems.at[swap_sem(t, h)])
    wait(start_send, send_sems.at[START])
    wait(early_send, send_sems.at[EARLY])
    wait(stage, send_sems.at[MATRIX])
    wait(step_send, send_sems.at[STEP])
    x_done.wait()
    wait(last_recv.at[pl.ds(0, chips - 1)], recv_sems.at[LAST])
    total = fold(1, chips, lambda d, total: total + last_recv[d], last_recv[0])
    sums = jnp.concatenate([total[:, :AREAS], total[:, AREAS:]], axis=0)
    price = sums / sums[s:s + 1]
    price_out[...] = price[:s]
    ends = sums[s + 1:s + 2] + small_eps
    weight_out[...] = jnp.sqrt(ends[:, sp:sp + s] / ends[:, :s])

    wait(last_recv.at[pl.ds(0, chips - 1)], send_sems.at[LAST])
    y_done.wait()


def hand_on(*refs):
    count = len(refs) // 2
    for i in range(count):
        refs[count + i][...] = refs[i][...]


def per_device(n, tiles, column_ids, costs, upper, demand, x_start, y_start, row_weight, area):
    s = costs.shape[1]
    hp = -(-(s + 2) // 32) * 16
    sp = 2 * hp
    chips = n // 2
    if n % 2 or chips & (chips - 1) or chips < 4 or tiles.shape[0] != 1:
        raise ValueError("unsupported mesh")
    f32 = jnp.float32
    vmem = pl.BlockSpec(memory_space=pltpu.VMEM)
    anywhere = pl.BlockSpec(memory_space=pltpu.HBM)
    phases = 8 * ITERS + 5
    by_case = [jnp.transpose(a, (1, 0, 2)) for a in (costs, upper, demand, x_start, y_start)]
    results = pl.pallas_call(
        functools.partial(kernel, n),
        out_shape=(
            jax.ShapeDtypeStruct((s, 1, LANES), f32),
            jax.ShapeDtypeStruct((s, 1, LANES), f32),
            jax.ShapeDtypeStruct((s, AREAS), f32),
            jax.ShapeDtypeStruct((1, s), f32),
        ),
        in_specs=[anywhere] * 9,
        out_specs=[anywhere] * 2 + [vmem] * 2,
        scratch_shapes=[
            pltpu.VMEM(tiles.shape[1:], jnp.bfloat16),
            pltpu.SMEM(column_ids.shape, jnp.int32),
            pltpu.VMEM((5, sp, LANES), f32),
            pltpu.VMEM((1, LANES), f32),
            pltpu.VMEM((1, LANES), jnp.int32),
            pltpu.VMEM((2, sp, LANES), f32),
            pltpu.VMEM((2 * LANES, chips * LANES), jnp.bfloat16),
            pltpu.VMEM((chips * LANES, 2 * LANES), jnp.bfloat16),
            pltpu.VMEM((LANES, chips * LANES), jnp.bfloat16),
            pltpu.VMEM((2, sp, LANES), f32),
            pltpu.VMEM((2, sp, LANES), f32),
            pltpu.VMEM((ITERS, 2, chips, hp, LANES), f32),
            pltpu.VMEM((ITERS, 2, chips, hp, LANES), f32),
            pltpu.VMEM((ITERS, 2, chips, hp, LANES), jnp.bfloat16),
            pltpu.VMEM((2, chips, hp, LANES), f32),
            pltpu.VMEM((2, chips, hp, LANES), f32),
            pltpu.VMEM((ITERS, 2, 2, hp, LANES), f32),
            pltpu.VMEM((ITERS, 2, 2, hp, LANES), f32),
            pltpu.VMEM((8, LANES), f32),
            pltpu.VMEM((8, LANES), f32),
            pltpu.VMEM((sp // 2, LANES), f32),
            pltpu.VMEM((chips, sp // 2, LANES), f32),
            pltpu.SemaphoreType.DMA((9,)),
            pltpu.SemaphoreType.DMA((phases,)),
            pltpu.SemaphoreType.DMA((phases,)),
        ],
        compiler_params=pltpu.CompilerParams(
            collective_id=0, has_side_effects=True, vmem_limit_bytes=60 * 2**20
        ),
    )(tiles, column_ids, *by_case, row_weight, area.reshape(1, -1))
    x_avg, y_avg, price, weight = pl.pallas_call(
        hand_on,
        out_shape=tuple(jax.ShapeDtypeStruct(a.shape, a.dtype) for a in results),
        in_specs=[vmem] * 4,
        out_specs=[vmem] * 4,
        compiler_params=pltpu.CompilerParams(vmem_limit_bytes=60 * 2**20),
    )(*results)
    x_avg, y_avg = (jnp.transpose(a, (1, 0, 2)) for a in (x_avg, y_avg))
    return x_avg, y_avg, price.T, weight.reshape(s)


def solution(mesh):
    case = P(("groups", "rows"), None, None)
    in_specs = (
        P("rows", None, None, None), P("rows", None), case, case, case, case, case,
        P("rows", None), P("rows"),
    )
    out_specs = (case, case, P("groups", None), P("groups"))
    return jax.shard_map(
        functools.partial(per_device, mesh.shape["rows"]),
        mesh=mesh, in_specs=in_specs, out_specs=out_specs, check_vma=False,
    )
```
